32 devices in a mesh: seq: 8 (over z, x), head: 4 (over y, core).
Axes of the slice: x: 2, y: 2, z: 4, core: 2. Of those that a mesh axis runs over, the one named last changes fastest.
Arguments:
- queries: bfloat16 [1024, 16, 64], P('seq', 'head'), may hold values from -6 to 6
- keys_values: bfloat16 [1024, 16, 128], P('seq', 'head'), may hold values from -6 to 6
- out_weight: bfloat16 [16, 64, 4096], P('head'), may hold values from -1 to 1
- out_grad: bfloat16 [1024, 4096], P('seq'), may hold values from -0.75 to 0.75
- block_order: int32 [8], replicated, may hold values from 0 to 7, each once
Outputs:
- mixed_out: bfloat16 [1024, 4096], P('seq', 'head')
- grad_queries: bfloat16 [1024, 16, 64], P('seq', 'head')
- grad_keys_values: bfloat16 [1024, 16, 128], P('seq', 'head')
The draws below stay inside these ranges and needn't reach their ends.
Inputs may be any that keep to these rules, and one draw needn't show every extreme that they name: `block_order`: A permutation of the sequence blocks 0 to 7.
All inputs are finite; a program needn't handle non-finite values.
Results may differ from the reference program's by a relative error of at most 0.03.
Values may be sent and summed in bfloat16 or wider, within the bound.
A program may use at most 64 MiB of HBM per device.

```python
import math
import jax
import jax.numpy as jnp
from jax import lax

D = 4096
H = 16
HD = 64
TOK_DEV = 128
TOKENS = 1024
N_SEQ = 8


def drawn_normal(key):
    return jnp.clip(jax.random.normal(key, (TOKENS, H, HD), jnp.float32), -4.5, 4.5)


def draw_queries(key, part):
    return drawn_normal(jax.random.fold_in(key, 1)).astype(jnp.bfloat16)


def draw_keys_values(key, part):
    keys_part = drawn_normal(jax.random.fold_in(key, 2))
    values_part = drawn_normal(jax.random.fold_in(key, 3))
    return jnp.concatenate([keys_part, values_part], axis=2).astype(jnp.bfloat16)


def strengthened(entries, key, source, target, blocks, factor):
    def block_of(axis_at):
        return (jnp.arange(entries.shape[axis_at]) // (entries.shape[axis_at] // blocks)).reshape((-1,) + (1,) * (entries.ndim - 1 - axis_at))

    first = jax.random.permutation(key, blocks)[block_of(target)]
    second = (block_of(target) + blocks // 2) % blocks
    return jnp.where((block_of(source) == first) | (block_of(source) == second), factor * entries, entries)


def shard_levels(rng, extent, pieces, smallest, high):
    def one(dim, parts):
        steps = jax.random.uniform(jax.random.fold_in(jax.random.fold_in(rng, 6), dim), (parts,), jnp.float32, smallest / len(pieces), high / len(pieces))
        return jnp.repeat(jnp.exp(steps), extent[dim] // parts).reshape((-1,) + (1,) * (len(extent) - dim - 1))

    factor_of = one(*pieces[0])
    for cut in pieces[1:]:
        factor_of = factor_of * one(*cut)
    return factor_of


def normal_values(own_key, extent, width, most, cuts=(), kind=jnp.bfloat16):
    entries = jax.random.normal(own_key, extent, jnp.float32) * width
    if len(cuts) > 0:
        entries = shard_levels(own_key, extent, cuts, -0.22, 0.18) * entries
    return jnp.clip(entries, min=-most, max=most).astype(kind)


def gaussian_with(key, dims, scale, reach, cuts, heavy, held_as=jnp.bfloat16):
    drawn = scale * jax.random.normal(key, dims, jnp.float32)
    if cuts:
        drawn = drawn * shard_levels(key, dims, cuts, -0.22, 0.18)
    return jnp.clip(strengthened(drawn, jax.random.fold_in(key, 3), *heavy), -reach, reach).astype(held_as)


def setup_inputs(seed: int = 0) -> dict:
    seeds = jax.random.split(jax.random.key(seed), 6)
    return {
        "queries": draw_queries(jax.random.fold_in(seeds[5], 71), 0),
        "keys_values": draw_keys_values(jax.random.fold_in(seeds[5], 71), 0),
        "out_weight": gaussian_with(seeds[2], (H, HD, D), HD ** -0.5, 1.0, ((0, 4),), (0, 2, 4, 2.0)),
        "out_grad": normal_values(seeds[3], (TOKENS, D), 0.125, 0.75, ((0, 8),)),
        "block_order": jax.random.permutation(seeds[4], N_SEQ).astype(jnp.int32),
    }


def log_normalizer(scores, allowed):
    masked = jnp.where(allowed, scores, -jnp.inf)
    row_max = lax.optimization_barrier(jnp.max(masked, axis=-1, keepdims=True))
    row_total = lax.optimization_barrier(jnp.sum(jnp.exp(masked - row_max), axis=-1, keepdims=True))
    return row_max + jnp.log(row_total)

def reference(queries, keys_values, out_weight, out_grad, block_order):
    tok_index = jnp.arange(TOKENS, dtype=jnp.int32)
    position = block_order[tok_index // TOK_DEV] * TOK_DEV + tok_index % TOK_DEV
    allowed = position[None, :] <= position[:, None]
    inv_root = 1.0 / math.sqrt(HD)

    def one_head(carry, inputs):
        query_head, kv_head, weight_head = inputs
        key_head = kv_head[:, :HD]
        value_head = kv_head[:, HD:]
        scores = jnp.dot(query_head, key_head.T, preferred_element_type=jnp.float32) * inv_root
        log_total = log_normalizer(scores, allowed)
        probs_low = jnp.where(allowed, jnp.exp(scores - log_total), 0.0).astype(jnp.bfloat16)
        attended = jnp.dot(probs_low, value_head, preferred_element_type=jnp.float32).astype(jnp.bfloat16)
        carry = carry + jnp.dot(attended, weight_head, preferred_element_type=jnp.float32)
        grad_att = jnp.dot(out_grad, weight_head.T, preferred_element_type=jnp.float32).astype(jnp.bfloat16)
        grad_dot = lax.optimization_barrier(jnp.sum(grad_att.astype(jnp.float32) * attended.astype(jnp.float32), axis=1, keepdims=True))
        dprob = jnp.dot(grad_att, value_head.T, preferred_element_type=jnp.float32)
        dscore = (probs_low.astype(jnp.float32) * (dprob - grad_dot)).astype(jnp.bfloat16)
        grad_query = (jnp.dot(dscore, key_head, preferred_element_type=jnp.float32) * inv_root).astype(jnp.bfloat16)
        grad_key = jnp.dot(dscore.T, query_head, preferred_element_type=jnp.float32) * inv_root
        grad_value = jnp.dot(probs_low.T, grad_att, preferred_element_type=jnp.float32)
        grad_kv = jnp.concatenate([grad_key, grad_value], axis=1).astype(jnp.bfloat16)
        return (carry, (grad_query, grad_kv))
    start = jnp.zeros((TOKENS, D), jnp.float32)
    inputs = (jnp.transpose(queries, (1, 0, 2)), jnp.transpose(keys_values, (1, 0, 2)), out_weight)
    summed, stacked = lax.scan(one_head, start, inputs)
    grad_queries = jnp.transpose(stacked[0], (1, 0, 2))
    grad_keys_values = jnp.transpose(stacked[1], (1, 0, 2))
    return (summed.astype(jnp.bfloat16), grad_queries, grad_keys_values)
```

```python
import functools
import math

import jax
import jax.numpy as jnp
from jax import lax
from jax.experimental import pallas as pl
from jax.experimental.pallas import tpu as pltpu
from jax.sharding import PartitionSpec as P

MESH = pl.DeviceIdType.MESH
F32 = jnp.float32
BF16 = jnp.bfloat16


def dot(a, b, dims=((1,), (0,))):
    return lax.dot_general(a, b, (dims, ((), ())), preferred_element_type=F32)


NT = ((1,), (1,))


def fused(
    n, nh, hh, rows, width, inv_root,
    q_ref, kv_ref, w_hbm, og_hbm, order_ref,
    mixed_ref, dq_ref, dkv_ref,
    w_ref, og_ref, kvbuf, stage, qgbuf, wbuf, probs, dscore,
    att_out, attbuf, dq_out, dqbuf, dkv_out, dkvbuf, attfull,
    local_sem, kv_s, kv_r, w_s, w_r, qg_s, qg_r, att_s, att_r, dq_s, dq_r, dkv_s, dkv_r,
):
    reps = n // hh
    half = rows // 2
    lanes = 2 * width
    me = lax.axis_index("seq")
    mh = lax.axis_index("head")
    my_z = me // reps
    cols = mixed_ref.shape[1]

    get_w = pltpu.make_async_copy(w_hbm, w_ref, local_sem.at[0])
    get_og = pltpu.make_async_copy(og_hbm, og_ref, local_sem.at[1])
    get_w.start()
    get_og.start()

    def seq_at(k):
        return lax.rem(me + (k + n), n)

    def head_at(k):
        return lax.rem(mh + (k + nh), nh)

    barrier = pltpu.get_barrier_semaphore()
    count = 0
    for k in range(1, n):
        pl.semaphore_signal(barrier, inc=1, device_id=(seq_at(k), mh), device_id_type=MESH)
        count += 1
    for j in range(hh):
        for d in range(1, nh):
            pl.semaphore_signal(
                barrier, inc=1, device_id=(seq_at(reps * j), head_at(d)), device_id_type=MESH
            )
            count += 1
    pl.semaphore_wait(barrier, count)

    sends = []

    def send(src, dst, send_sem, recv_sem, seq, head):
        copy = pltpu.make_async_remote_copy(
            src_ref=src, dst_ref=dst, send_sem=send_sem, recv_sem=recv_sem,
            device_id=(seq, head), device_id_type=MESH,
        )
        copy.start()
        sends.append(copy)

    def arrived(dst, send_sem, recv_sem):
        pltpu.make_async_remote_copy(
            src_ref=dst, dst_ref=dst, send_sem=send_sem, recv_sem=recv_sem,
            device_id=(seq_at(1), mh), device_id_type=MESH,
        ).wait_recv()

    def lane_block(i, size):
        return pl.ds(pl.multiple_of(i * size, size), size)

    for k in range(1, n):
        to = seq_at(k)
        send(
            kv_ref.at[:, lane_block(to // reps, lanes)], kvbuf.at[pl.ds(k * rows, rows)],
            kv_s.at[k], kv_r.at[k], to, mh,
        )
    kvbuf[0:rows, :] = kv_ref[:, lane_block(my_z, lanes)]
    for d in range(nh - 1, 0, -1):
        to = head_at(d)
        send(w_hbm.at[:, lane_block(to, cols)], wbuf.at[d], w_s.at[d], w_r.at[d], me, to)

    low = lax.broadcasted_iota(jnp.int32, (rows, lanes), 1) < width
    low_half = low[:half]

    get_w.wait()
    get_og.wait()
    gatt = dot(og_ref[...], w_ref[...], NT)
    for pair in range(hh // 2):
        at = slice(pair * lanes, (pair + 1) * lanes)
        q_pair = q_ref[:, at].astype(F32)
        g_pair = gatt[:, at]
        stage[2 * pair] = jnp.where(low, q_pair, pltpu.roll(g_pair, width, 1)).astype(BF16)
        stage[2 * pair + 1] = jnp.where(low, pltpu.roll(q_pair, width, 1), g_pair).astype(BF16)
    for j in range(1, hh):
        to = seq_at(reps * j)
        send(stage.at[to // reps], qgbuf.at[j], qg_s.at[j], qg_r.at[j], to, mh)
    qgbuf[0] = stage[my_z]

    offsets = lax.broadcasted_iota(jnp.int32, (1, rows), 1)
    key_pos = jnp.concatenate(
        [order_ref[seq_at(-k)] * rows + offsets for k in range(n)], axis=1
    )
    row_iota = lax.broadcasted_iota(jnp.int32, (rows, 1), 0)

    def pack(x):
        return jnp.where(low_half, x[:half], pltpu.roll(x[half:], width, 1)).astype(BF16)

    def pack_high(x):
        return jnp.where(low_half, pltpu.roll(x[:half], width, 1), x[half:]).astype(BF16)

    for k in range(1, n):
        arrived(kvbuf.at[pl.ds(k * rows, rows)], kv_s.at[k], kv_r.at[k])

    for j in range(hh):
        owner = seq_at(-reps * j)
        if j > 0:
            arrived(qgbuf.at[j], qg_s.at[j], qg_r.at[j])
        qg = qgbuf[j]
        zero = jnp.zeros_like(qg)
        kv = kvbuf[...]
        scores = dot(jnp.where(low, qg, zero), kv, NT) * inv_root
        allowed = key_pos <= order_ref[owner] * rows + row_iota
        scores = jnp.where(allowed, scores, -jnp.inf)
        e = jnp.exp(scores - jnp.max(scores, axis=1, keepdims=True))
        p = (e * (1.0 / jnp.sum(e, axis=1, keepdims=True))).astype(BF16)
        probs[j * rows:(j + 1) * rows, :] = p
        att = dot(p, kv)
        att_out[j] = pack_high(att)
        for d in range(nh):
            if d == 0 and j == 0:
                attbuf[0, my_z] = att_out[0]
            else:
                send(
                    att_out.at[j], attbuf.at[d, my_z], att_s.at[d, j], att_r.at[d, j],
                    owner, head_at(d),
                )
        dprob = dot(jnp.where(low, zero, qg), kv, NT)
        grad_dot = jnp.sum(
            jnp.where(low, 0.0, qg.astype(F32) * att.astype(BF16).astype(F32)),
            axis=1, keepdims=True,
        )
        ds = (p.astype(F32) * (dprob - grad_dot)).astype(BF16)
        dscore[j * rows:(j + 1) * rows, :] = ds
        dq_out[j] = pack(dot(ds, kv) * inv_root)
        if j == 0:
            dqbuf[my_z] = dq_out[0]
        else:
            send(dq_out.at[j], dqbuf.at[my_z], dq_s.at[j], dq_r.at[j], owner, mh)

    qg_all = qgbuf[...].reshape(hh * rows, lanes)
    qgt = jnp.transpose(qg_all.astype(F32)).astype(BF16)
    grad_k = dot(qgt, dscore[...]) * inv_root
    grad_v = dot(qgt, probs[...])
    upper = lax.broadcasted_iota(jnp.int32, (lanes, rows), 0) < width
    for k in [*range(1, n), 0]:
        at = slice(k * rows, (k + 1) * rows)
        dkv_out[k] = jnp.transpose(jnp.where(upper, grad_k[:, at], grad_v[:, at])).astype(BF16)
        if k == 0:
            dkvbuf[0] = dkv_out[0]
        else:
            send(dkv_out.at[k], dkvbuf.at[k], dkv_s.at[k], dkv_r.at[k], seq_at(-k), mh)

    def unpack(first, second):
        first, second = first.astype(F32), second.astype(F32)
        top = jnp.where(low_half, first, pltpu.roll(second, width, 1)).astype(BF16)
        bottom = jnp.where(low_half, pltpu.roll(first, width, 1), second).astype(BF16)
        return top, bottom

    for j in range(1, hh):
        arrived(dqbuf.at[(my_z + j) % hh], dq_s.at[j], dq_r.at[j])
    for pair in range(hh // 2):
        at = slice(pair * lanes, (pair + 1) * lanes)
        top, bottom = unpack(dqbuf[2 * pair], dqbuf[2 * pair + 1])
        dq_ref[0:half, at] = top
        dq_ref[half:rows, at] = bottom

    total = None
    for d in range(nh):
        for j in range(hh):
            if d or j:
                arrived(attbuf.at[d, (my_z + j) % hh], att_s.at[d, j], att_r.at[d, j])
        for pair in range(hh // 2):
            at = slice(pair * lanes, (pair + 1) * lanes)
            top, bottom = unpack(attbuf[d, 2 * pair], attbuf[d, 2 * pair + 1])
            attfull[d, 0:half, at] = top
            attfull[d, half:rows, at] = bottom
        if d == 0:
            weight = w_ref[:, lane_block(mh, cols)]
        else:
            arrived(wbuf.at[d], w_s.at[d], w_r.at[d])
            weight = wbuf[d]
        term = dot(attfull[d], weight)
        total = term if total is None else total + term
    mixed_ref[...] = total.astype(BF16)

    for k in range(1, n):
        arrived(dkvbuf.at[k], dkv_s.at[k], dkv_r.at[k])
    for z in range(hh):
        acc = None
        for r in range(reps):
            term = dkvbuf[lax.rem(z * reps + r + n - me, n)].astype(F32)
            acc = term if acc is None else acc + term
        dkv_ref[:, z * lanes:(z + 1) * lanes] = acc.astype(BF16)

    for copy in sends:
        copy.wait_send()


def fused_local(n, nh, queries, keys_values, out_weight, out_grad, block_order):
    rows, hh, width = queries.shape
    lanes = 2 * width
    depth = out_grad.shape[1]
    cols = depth // nh
    half = rows // 2
    vmem = pl.BlockSpec(memory_space=pltpu.VMEM)
    hbm = pl.BlockSpec(memory_space=pl.ANY)
    dma = pltpu.SemaphoreType.DMA
    mixed, dq, dkv = pl.pallas_call(
        functools.partial(fused, n, nh, hh, rows, width, 1.0 / math.sqrt(width)),
        out_shape=(
            jax.ShapeDtypeStruct((rows, cols), BF16),
            jax.ShapeDtypeStruct((rows, hh * width), BF16),
            jax.ShapeDtypeStruct((rows, hh * lanes), BF16),
        ),
        in_specs=[vmem, vmem, hbm, hbm, pl.BlockSpec(memory_space=pltpu.SMEM)],
        out_specs=(vmem, vmem, vmem),
        scratch_shapes=[
            pltpu.VMEM((hh * width, depth), BF16),
            pltpu.VMEM((rows, depth), BF16),
            pltpu.VMEM((n * rows, lanes), BF16),
            pltpu.VMEM((hh, rows, lanes), BF16),
            pltpu.VMEM((hh, rows, lanes), BF16),
            pltpu.VMEM((nh, hh * width, cols), BF16),
            pltpu.VMEM((hh * rows, n * rows), BF16),
            pltpu.VMEM((hh * rows, n * rows), BF16),
            pltpu.VMEM((hh, half, lanes), BF16),
            pltpu.VMEM((nh, hh, half, lanes), BF16),
            pltpu.VMEM((hh, half, lanes), BF16),
            pltpu.VMEM((hh, half, lanes), BF16),
            pltpu.VMEM((n, rows, lanes), BF16),
            pltpu.VMEM((n, rows, lanes), BF16),
            pltpu.VMEM((nh, rows, hh * width), BF16),
            dma((2,)),
            dma((n,)), dma((n,)),
            dma((nh,)), dma((nh,)),
            dma((hh,)), dma((hh,)),
            dma((nh, hh)), dma((nh, hh)),
            dma((hh,)), dma((hh,)),
            dma((n,)), dma((n,)),
        ],
        compiler_params=pltpu.CompilerParams(
            collective_id=0, has_side_effects=True, vmem_limit_bytes=48 * 2**20
        ),
    )(
        queries.reshape(rows, hh * width),
        keys_values.reshape(rows, hh * lanes),
        out_weight.reshape(hh * width, depth),
        out_grad,
        block_order,
    )
    return mixed, dq.reshape(queries.shape), dkv.reshape(keys_values.shape)


def log_normalizer(scores, allowed):
    masked = jnp.where(allowed, scores, -jnp.inf)
    row_max = jnp.max(masked, axis=-1, keepdims=True)
    row_total = jnp.sum(jnp.exp(masked - row_max), axis=-1, keepdims=True)
    return (row_max + jnp.log(row_total))[..., 0]


def local(queries, keys_values, out_weight, out_grad, block_order):
    tok_rows = queries.shape[0]
    head_width = queries.shape[2]
    inv_root = 1.0 / math.sqrt(head_width)
    my_block = block_order[lax.axis_index("seq")]
    offsets = jnp.arange(tok_rows, dtype=jnp.int32)
    my_position = my_block * tok_rows + offsets
    all_position = (block_order[:, None] * tok_rows + offsets[None, :]).reshape(-1)
    gathered = lax.all_gather(keys_values, "seq", axis=0, tiled=True)
    all_keys = gathered[:, :, :head_width]
    all_values = gathered[:, :, head_width:]
    allowed = (all_position[None, :] <= my_position[:, None])[None]
    scores = (
        jnp.einsum("qhd,khd->hqk", queries, all_keys, preferred_element_type=jnp.float32) * inv_root
    )
    log_total = log_normalizer(scores, allowed)
    probs_low = jnp.where(allowed, jnp.exp(scores - log_total[:, :, None]), 0.0).astype(
        jnp.bfloat16
    )
    attended = jnp.einsum(
        "hqk,khd->qhd", probs_low, all_values, preferred_element_type=jnp.float32
    ).astype(jnp.bfloat16)
    partial_value = jnp.einsum(
        "qhd,hde->qe", attended, out_weight, preferred_element_type=jnp.float32
    )
    mixed_out = lax.psum_scatter(partial_value, "head", scatter_dimension=1, tiled=True).astype(
        jnp.bfloat16
    )
    grad_att = jnp.einsum(
        "qe,hde->qhd", out_grad, out_weight, preferred_element_type=jnp.float32
    ).astype(jnp.bfloat16)
    grad_dot = jnp.sum(grad_att.astype(jnp.float32) * attended.astype(jnp.float32), axis=2)
    dprob = jnp.einsum("qhd,khd->hqk", grad_att, all_values, preferred_element_type=jnp.float32)
    dscore = (probs_low.astype(jnp.float32) * (dprob - grad_dot.T[:, :, None])).astype(jnp.bfloat16)
    grad_queries = (
        jnp.einsum("hqk,khd->qhd", dscore, all_keys, preferred_element_type=jnp.float32) * inv_root
    ).astype(jnp.bfloat16)
    grad_keys = (
        jnp.einsum("hqk,qhd->khd", dscore, queries, preferred_element_type=jnp.float32) * inv_root
    )
    grad_values = jnp.einsum(
        "hqk,qhd->khd", probs_low, grad_att, preferred_element_type=jnp.float32
    )
    terms = jnp.concatenate([grad_keys, grad_values], axis=2)
    summed = lax.psum_scatter(terms, "seq", scatter_dimension=0, tiled=True)
    grad_keys_values = summed.astype(jnp.bfloat16)
    return (mixed_out, grad_queries, grad_keys_values)


def solution(mesh):
    n, nh = mesh.shape["seq"], mesh.shape["head"]

    def step(queries, keys_values, out_weight, out_grad, block_order):
        rows, hh, width = queries.shape
        fits = hh % 2 == 0 and n % hh == 0 and 2 * width == 128 and rows % 32 == 0
        if fits and 8 * n * rows * hh * rows < 2**23:
            return fused_local(n, nh, queries, keys_values, out_weight, out_grad, block_order)
        return local(queries, keys_values, out_weight, out_grad, block_order)

    return jax.shard_map(
        step,
        mesh=mesh,
        in_specs=(
            P("seq", "head", None),
            P("seq", "head", None),
            P("head", None, None),
            P("seq", None),
            P(),
        ),
        out_specs=(P("seq", "head"), P("seq", "head", None), P("seq", "head", None)),
        check_vma=False,
    )
```

```python
import functools
import math

import jax
import jax.numpy as jnp
from jax import lax
from jax.experimental import pallas as pl
from jax.experimental.pallas import tpu as pltpu
from jax.sharding import PartitionSpec as P

MESH = pl.DeviceIdType.MESH
F32 = jnp.float32
BF16 = jnp.bfloat16
PIECES = 2


def dot(a, b, dims=((1,), (0,))):
    return lax.dot_general(a, b, (dims, ((), ())), preferred_element_type=F32)


NT = ((1,), (1,))


def fused(
    n, nh, hh, rows, width, inv_root,
    q_hbm, kv_hbm, w_hbm, og_hbm, order_ref,
    mixed_ref, dq_ref, dkv_ref,
    q_ref, kv_ref, w_ref, og_ref, kvstage, kvbuf, kvt, stage, qgbuf, wbuf, probs, dscore,
    att_out, attbuf, dq_out, dqbuf, dkv_out, dkvbuf,
    local_sem, kv_s, kv_r, w_s, w_r, f_s, f_r,
    qg_s, qg_r, att_s, att_r, dq_s, dq_r, dkv_s, dkv_r,
):
    reps = n // hh
    lanes = 2 * width
    me = lax.axis_index("seq")
    mh = lax.axis_index("head")
    my_z = me // reps
    my_r = lax.rem(me, reps)
    my_y, my_c = mh // 2, lax.rem(mh, 2)
    n_y = nh // 2
    cols = mixed_ref.shape[1]
    w_rows = hh * width
    share = w_rows // reps
    piece = share // PIECES

    loads = [
        pltpu.make_async_copy(src, dst, local_sem.at[i])
        for i, (src, dst) in enumerate(
            [(kv_hbm, kv_ref), (w_hbm, w_ref), (og_hbm, og_ref), (q_hbm, q_ref)]
        )
    ]
    for load in loads:
        load.start()

    def seq_at(k):
        return lax.rem(me + (k + n), n)

    def head_at(d, sign=1):
        y = lax.rem(my_y + (sign * (d // 2) + n_y), n_y)
        return y * 2 + lax.rem(my_c + d % 2, 2)

    def side_at(r):
        return my_z * reps + lax.rem(my_r + (r + reps), reps)

    barrier = pltpu.get_barrier_semaphore()
    count = 0
    for k in range(1, n):
        pl.semaphore_signal(barrier, inc=1, device_id=(seq_at(k), mh), device_id_type=MESH)
        count += 1
    for j in range(hh):
        for d in range(1, nh):
            pl.semaphore_signal(
                barrier, inc=1, device_id=(seq_at(reps * j), head_at(d, -1)), device_id_type=MESH
            )
            count += 1
    loads[0].wait()
    for z in range(hh):
        kvstage[z] = kv_ref[:, z, :]
    pl.semaphore_wait(barrier, count)

    sends = []

    def send(src, dst, send_sem, recv_sem, seq, head):
        copy = pltpu.make_async_remote_copy(
            src_ref=src, dst_ref=dst, send_sem=send_sem, recv_sem=recv_sem,
            device_id=(seq, head), device_id_type=MESH,
        )
        copy.start()
        sends.append(copy)

    def arrived(dst, send_sem, recv_sem):
        pltpu.make_async_remote_copy(
            src_ref=dst, dst_ref=dst, send_sem=send_sem, recv_sem=recv_sem,
            device_id=(seq_at(1), mh), device_id_type=MESH,
        ).wait_recv()

    def w_part(r, i):
        return pl.ds(pl.multiple_of(r * share + i * piece, piece), piece)

    for k in range(1, n):
        to = seq_at(k)
        send(
            kvstage.at[to // reps], kvbuf.at[pl.ds(k * rows, rows)],
            kv_s.at[k], kv_r.at[k], to, mh,
        )
    far = [(i, d) for i in range(PIECES) for d in range(2, nh)]
    for i, d in far:
        to = head_at(d)
        at = pl.ds(pl.multiple_of(to * cols, cols), cols)
        send(
            w_hbm.at[w_part(my_r, i), at], wbuf.at[d, w_part(my_r, i)],
            w_s.at[d, i], w_r.at[d, i], me, to,
        )
    at = pl.ds(pl.multiple_of(head_at(1) * cols, cols), cols)
    send(w_hbm.at[:, at], wbuf.at[1], w_s.at[1, 0], w_r.at[1, 0], me, head_at(1))

    def forward(i, d):
        part = wbuf.at[d, w_part(my_r, i)]
        arrived(part, w_s.at[d, i], w_r.at[d, i])
        for r in range(1, reps):
            send(part, part, f_s.at[d, i, r], f_r.at[d, i, r], side_at(r), mh)

    kvbuf[0:rows, :] = kvstage[my_z]
    kvt[:, 0:rows] = jnp.transpose(kvstage[my_z].astype(F32)).astype(BF16)

    loads[1].wait()
    loads[2].wait()
    loads[3].wait()
    gatt = dot(w_ref[...], og_ref[...], NT).astype(BF16)
    for z in range(hh):
        at = slice(z * width, (z + 1) * width)
        stage[z, 0:width] = q_ref[at]
        stage[z, width:lanes] = gatt[at]
    for j in range(1, hh):
        to = seq_at(reps * j)
        send(stage.at[to // reps], qgbuf.at[j], qg_s.at[j], qg_r.at[j], to, mh)
    qgbuf[0] = stage[my_z]

    offsets = lax.broadcasted_iota(jnp.int32, (1, rows), 1)
    key_pos = jnp.concatenate(
        [order_ref[seq_at(-k)] * rows + offsets for k in range(n)], axis=1
    )
    row_iota = lax.broadcasted_iota(jnp.int32, (rows, 1), 0)
    low = lax.broadcasted_iota(jnp.int32, (rows, lanes), 1) < width

    for step, (i, d) in enumerate(far):
        if step < len(far) // 2:
            forward(i, d)
    for k in range(1, n):
        at = slice(k * rows, (k + 1) * rows)
        arrived(kvbuf.at[pl.ds(k * rows, rows)], kv_s.at[k], kv_r.at[k])
        kvt[:, at] = jnp.transpose(kvbuf[at, :].astype(F32)).astype(BF16)
    ahead = far[len(far) // 2:]

    for j in range(hh):
        owner = seq_at(-reps * j)
        if j > 0:
            arrived(qgbuf.at[j], qg_s.at[j], qg_r.at[j])
        qg = jnp.transpose(qgbuf[j].astype(F32))
        grad_rows = jnp.where(low, 0.0, qg)
        scores = dot(jnp.where(low, qg, 0.0).astype(BF16), kvt[...]) * inv_root
        allowed = key_pos <= order_ref[owner] * rows + row_iota
        scores = jnp.where(allowed, scores, -jnp.inf)
        e = jnp.exp(scores - jnp.max(scores, axis=1, keepdims=True))
        p = (e * (1.0 / jnp.sum(e, axis=1, keepdims=True))).astype(BF16)
        probs[j * rows:(j + 1) * rows, :] = p
        att = dot(p, kvbuf[...])
        att_out[j] = jnp.transpose(att)[width:].astype(BF16)
        my_rows = pl.ds(pl.multiple_of(my_z * width, width), width)
        for d in range(nh):
            if d == 0 and j == 0:
                attbuf[0, my_rows, :] = att_out[0]
            else:
                send(
                    att_out.at[j], attbuf.at[d, my_rows], att_s.at[d, j], att_r.at[d, j],
                    owner, head_at(d),
                )
        dprob = dot(grad_rows.astype(BF16), kvt[...])
        grad_dot = jnp.sum(grad_rows * att.astype(BF16).astype(F32), axis=1, keepdims=True)
        ds = (p.astype(F32) * (dprob - grad_dot)).astype(BF16)
        dscore[j * rows:(j + 1) * rows, :] = ds
        dq_out[j] = jnp.transpose(dot(ds, kvbuf[...]) * inv_root)[:width].astype(BF16)
        if j == 0:
            dqbuf[my_rows, :] = dq_out[0]
        else:
            send(dq_out.at[j], dqbuf.at[my_rows], dq_s.at[j], dq_r.at[j], owner, mh)
        for i, d in ahead[j * len(ahead) // hh:(j + 1) * len(ahead) // hh]:
            forward(i, d)

    qgt = jnp.concatenate([qgbuf[j] for j in range(hh)], axis=1)
    grad_k = dot(qgt, dscore[...]) * inv_root
    grad_v = dot(qgt, probs[...])
    upper = lax.broadcasted_iota(jnp.int32, (lanes, rows), 0) < width
    for k in [*range(1, n), 0]:
        at = slice(k * rows, (k + 1) * rows)
        dkv_out[k] = jnp.transpose(jnp.where(upper, grad_k[:, at], grad_v[:, at])).astype(BF16)
        if k == 0:
            dkvbuf[0] = dkv_out[0]
        else:
            send(dkv_out.at[k], dkvbuf.at[k], dkv_s.at[k], dkv_r.at[k], seq_at(-k), mh)

    def z_rows(j):
        z = lax.rem(my_z + j, hh)
        return pl.ds(pl.multiple_of(z * width, width), width)

    for j in range(1, hh):
        arrived(dqbuf.at[z_rows(j)], dq_s.at[j], dq_r.at[j])
    dq_ref[...] = dqbuf[...]

    total = None
    for d in range(nh):
        for j in range(hh):
            if d or j:
                arrived(attbuf.at[d, z_rows(j)], att_s.at[d, j], att_r.at[d, j])
        if d == 0:
            weight = w_ref[:, pl.ds(pl.multiple_of(mh * cols, cols), cols)]
        else:
            if d == 1:
                arrived(wbuf.at[1], w_s.at[1, 0], w_r.at[1, 0])
            else:
                for i in range(PIECES):
                    for r in range(1, reps):
                        source = lax.rem(my_r + (reps - r), reps)
                        arrived(
                            wbuf.at[d, w_part(source, i)], f_s.at[d, i, r], f_r.at[d, i, r]
                        )
            weight = wbuf[d]
        att_rows = jnp.transpose(attbuf[d].astype(F32)).astype(BF16)
        term = dot(att_rows, weight)
        total = term if total is None else total + term
    mixed_ref[...] = total.astype(BF16)

    for k in range(1, n):
        arrived(dkvbuf.at[k], dkv_s.at[k], dkv_r.at[k])
    for z in range(hh):
        acc = None
        for r in range(reps):
            term = dkvbuf[lax.rem(z * reps + r + n - me, n)].astype(F32)
            acc = term if acc is None else acc + term
        dkv_ref[:, z, :] = acc.astype(BF16)

    for copy in sends:
        copy.wait_send()


def fused_local(n, nh, queries, keys_values, out_weight, out_grad, block_order):
    rows, hh, width = queries.shape
    lanes = 2 * width
    depth = out_grad.shape[1]
    cols = depth // nh
    reps = n // hh
    vmem = pl.BlockSpec(memory_space=pltpu.VMEM)
    hbm = pl.BlockSpec(memory_space=pl.ANY)
    dma = pltpu.SemaphoreType.DMA
    mixed, dq, dkv = pl.pallas_call(
        functools.partial(fused, n, nh, hh, rows, width, 1.0 / math.sqrt(width)),
        out_shape=(
            jax.ShapeDtypeStruct((rows, cols), BF16),
            jax.ShapeDtypeStruct((hh * width, rows), BF16),
            jax.ShapeDtypeStruct((rows, hh, lanes), BF16),
        ),
        in_specs=[hbm, hbm, hbm, hbm, pl.BlockSpec(memory_space=pltpu.SMEM)],
        out_specs=(vmem, vmem, vmem),
        scratch_shapes=[
            pltpu.VMEM((hh * width, rows), BF16),
            pltpu.VMEM((rows, hh, lanes), BF16),
            pltpu.VMEM((hh * width, depth), BF16),
            pltpu.VMEM((rows, depth), BF16),
            pltpu.VMEM((hh, rows, lanes), BF16),
            pltpu.VMEM((n * rows, lanes), BF16),
            pltpu.VMEM((lanes, n * rows), BF16),
            pltpu.VMEM((hh, lanes, rows), BF16),
            pltpu.VMEM((hh, lanes, rows), BF16),
            pltpu.VMEM((nh, hh * width, cols), BF16),
            pltpu.VMEM((hh * rows, n * rows), BF16),
            pltpu.VMEM((hh * rows, n * rows), BF16),
            pltpu.VMEM((hh, width, rows), BF16),
            pltpu.VMEM((nh, hh * width, rows), BF16),
            pltpu.VMEM((hh, width, rows), BF16),
            pltpu.VMEM((hh * width, rows), BF16),
            pltpu.VMEM((n, rows, lanes), BF16),
            pltpu.VMEM((n, rows, lanes), BF16),
            dma((4,)),
            dma((n,)), dma((n,)),
            dma((nh, PIECES)), dma((nh, PIECES)),
            dma((nh, PIECES, reps)), dma((nh, PIECES, reps)),
            dma((hh,)), dma((hh,)),
            dma((nh, hh)), dma((nh, hh)),
            dma((hh,)), dma((hh,)),
            dma((n,)), dma((n,)),
        ],
        compiler_params=pltpu.CompilerParams(
            collective_id=0, has_side_effects=True, vmem_limit_bytes=60 * 2**20
        ),
    )(
        jnp.transpose(queries, (1, 2, 0)).reshape(hh * width, rows),
        keys_values,
        out_weight.reshape(hh * width, depth),
        out_grad,
        block_order,
    )
    dq = jnp.transpose(dq.reshape(hh, width, rows), (2, 0, 1))
    return mixed, dq, dkv


def log_normalizer(scores, allowed):
    masked = jnp.where(allowed, scores, -jnp.inf)
    row_max = jnp.max(masked, axis=-1, keepdims=True)
    row_total = jnp.sum(jnp.exp(masked - row_max), axis=-1, keepdims=True)
    return (row_max + jnp.log(row_total))[..., 0]


def local(queries, keys_values, out_weight, out_grad, block_order):
    tok_rows = queries.shape[0]
    head_width = queries.shape[2]
    inv_root = 1.0 / math.sqrt(head_width)
    my_block = block_order[lax.axis_index("seq")]
    offsets = jnp.arange(tok_rows, dtype=jnp.int32)
    my_position = my_block * tok_rows + offsets
    all_position = (block_order[:, None] * tok_rows + offsets[None, :]).reshape(-1)
    gathered = lax.all_gather(keys_values, "seq", axis=0, tiled=True)
    all_keys = gathered[:, :, :head_width]
    all_values = gathered[:, :, head_width:]
    allowed = (all_position[None, :] <= my_position[:, None])[None]
    scores = (
        jnp.einsum("qhd,khd->hqk", queries, all_keys, preferred_element_type=jnp.float32) * inv_root
    )
    log_total = log_normalizer(scores, allowed)
    probs_low = jnp.where(allowed, jnp.exp(scores - log_total[:, :, None]), 0.0).astype(
        jnp.bfloat16
    )
    attended = jnp.einsum(
        "hqk,khd->qhd", probs_low, all_values, preferred_element_type=jnp.float32
    ).astype(jnp.bfloat16)
    partial_value = jnp.einsum(
        "qhd,hde->qe", attended, out_weight, preferred_element_type=jnp.float32
    )
    mixed_out = lax.psum_scatter(partial_value, "head", scatter_dimension=1, tiled=True).astype(
        jnp.bfloat16
    )
    grad_att = jnp.einsum(
        "qe,hde->qhd", out_grad, out_weight, preferred_element_type=jnp.float32
    ).astype(jnp.bfloat16)
    grad_dot = jnp.sum(grad_att.astype(jnp.float32) * attended.astype(jnp.float32), axis=2)
    dprob = jnp.einsum("qhd,khd->hqk", grad_att, all_values, preferred_element_type=jnp.float32)
    dscore = (probs_low.astype(jnp.float32) * (dprob - grad_dot.T[:, :, None])).astype(jnp.bfloat16)
    grad_queries = (
        jnp.einsum("hqk,khd->qhd", dscore, all_keys, preferred_element_type=jnp.float32) * inv_root
    ).astype(jnp.bfloat16)
    grad_keys = (
        jnp.einsum("hqk,qhd->khd", dscore, queries, preferred_element_type=jnp.float32) * inv_root
    )
    grad_values = jnp.einsum(
        "hqk,qhd->khd", probs_low, grad_att, preferred_element_type=jnp.float32
    )
    terms = jnp.concatenate([grad_keys, grad_values], axis=2)
    summed = lax.psum_scatter(terms, "seq", scatter_dimension=0, tiled=True)
    grad_keys_values = summed.astype(jnp.bfloat16)
    return (mixed_out, grad_queries, grad_keys_values)


def solution(mesh):
    n, nh = mesh.shape["seq"], mesh.shape["head"]

    def step(queries, keys_values, out_weight, out_grad, block_order):
        rows, hh, width = queries.shape
        fits = nh % 2 == 0 and n % hh == 0 and width == 64 and rows % 128 == 0
        if fits and 8 * n * rows * hh * rows < 2**23:
            return fused_local(n, nh, queries, keys_values, out_weight, out_grad, block_order)
        return local(queries, keys_values, out_weight, out_grad, block_order)

    return jax.shard_map(
        step,
        mesh=mesh,
        in_specs=(
            P("seq", "head", None),
            P("seq", "head", None),
            P("head", None, None),
            P("seq", None),
            P(),
        ),
        out_specs=(P("seq", "head"), P("seq", "head", None), P("seq", "head", None)),
        check_vma=False,
    )
```

```python
import functools
import math

import jax
import jax.numpy as jnp
from jax import lax
from jax.experimental import pallas as pl
from jax.experimental.pallas import tpu as pltpu
from jax.sharding import PartitionSpec as P

MESH = pl.DeviceIdType.MESH
F32 = jnp.float32
BF16 = jnp.bfloat16
PIECES = 2
VLIM = 952


def dot(a, b, dims=((1,), (0,))):
    return lax.dot_general(a, b, (dims, ((), ())), preferred_element_type=F32)


NT = ((1,), (1,))


def fused(
    n, nh, hh, rows, width, inv_root,
    q_hbm, kv_hbm, w_hbm, og_hbm, order_ref,
    mixed_ref, dq_ref, dkv_ref,
    q_ref, kv_ref, w_ref, og_ref, kvstage, kvbuf, kvt, stage, qgbuf, wbuf, probs, dscore,
    attbuf, home_out, homebuf, dkv_out, dkvbuf,
    local_sem, kv_s, kv_r, w_s, w_r, f_s, f_r,
    qg_s, qg_r, att_s, att_r, home_s, home_r, dkv_s, dkv_r,
):
    reps = n // hh
    lanes = 2 * width
    me = lax.axis_index("seq")
    mh = lax.axis_index("head")
    my_z = me // reps
    my_r = lax.rem(me, reps)
    my_y, my_c = mh // 2, lax.rem(mh, 2)
    n_y = nh // 2
    cols = mixed_ref.shape[1]
    w_rows = hh * width
    share = w_rows // reps
    piece = share // PIECES

    loads = [
        pltpu.make_async_copy(src, dst, local_sem.at[i])
        for i, (src, dst) in enumerate(
            [(kv_hbm, kv_ref), (w_hbm, w_ref), (og_hbm, og_ref), (q_hbm, q_ref)]
        )
    ]
    for load in loads:
        load.start()

    def seq_at(k):
        return lax.rem(me + (k + n), n)

    def head_at(d, sign=1):
        y = lax.rem(my_y + (sign * (d // 2) + n_y), n_y)
        return y * 2 + lax.rem(my_c + d % 2, 2)

    def side_at(r):
        return my_z * reps + lax.rem(my_r + (r + reps), reps)

    barrier = pltpu.get_barrier_semaphore()
    count = 0
    for k in range(1, n):
        pl.semaphore_signal(barrier, inc=1, device_id=(seq_at(k), mh), device_id_type=MESH)
        count += 1
    for d in range(1, nh):
        pl.semaphore_signal(barrier, inc=1, device_id=(me, head_at(d, -1)), device_id_type=MESH)
        count += 1
    loads[0].wait()
    for z in range(hh):
        kvstage[z] = kv_ref[:, z, :]
    pl.semaphore_wait(barrier, count)

    sends = []

    def send(src, dst, send_sem, recv_sem, seq, head):
        copy = pltpu.make_async_remote_copy(
            src_ref=src, dst_ref=dst, send_sem=send_sem, recv_sem=recv_sem,
            device_id=(seq, head), device_id_type=MESH,
        )
        copy.start()
        sends.append(copy)

    def arrived(dst, send_sem, recv_sem):
        pltpu.make_async_remote_copy(
            src_ref=dst, dst_ref=dst, send_sem=send_sem, recv_sem=recv_sem,
            device_id=(seq_at(1), mh), device_id_type=MESH,
        ).wait_recv()

    def w_part(r, i):
        return pl.ds(pl.multiple_of(r * share + i * piece, piece), piece)

    for k in range(1, n):
        to = seq_at(k)
        send(
            kvstage.at[to // reps], kvbuf.at[pl.ds(k * rows, rows)],
            kv_s.at[k], kv_r.at[k], to, mh,
        )
    far = [(i, d) for i in range(PIECES) for d in range(2, nh)]
    for i, d in far:
        to = head_at(d)
        at = pl.ds(pl.multiple_of(to * cols, cols), cols)
        send(
            w_hbm.at[w_part(my_r, i), at], wbuf.at[d, w_part(my_r, i)],
            w_s.at[d, i], w_r.at[d, i], me, to,
        )
    at = pl.ds(pl.multiple_of(head_at(1) * cols, cols), cols)
    send(w_hbm.at[:, at], wbuf.at[1], w_s.at[1, 0], w_r.at[1, 0], me, head_at(1))

    def forward(i, d):
        part = wbuf.at[d, w_part(my_r, i)]
        arrived(part, w_s.at[d, i], w_r.at[d, i])
        for r in range(1, reps):
            send(part, part, f_s.at[d, i, r], f_r.at[d, i, r], side_at(r), mh)

    kvbuf[0:rows, :] = kvstage[my_z]
    kvt[:, 0:rows] = jnp.transpose(kvstage[my_z].astype(F32)).astype(BF16)

    loads[1].wait()
    loads[2].wait()
    loads[3].wait()
    gatt = dot(w_ref[...], og_ref[...], NT).astype(BF16)
    for z in range(hh):
        at = slice(z * width, (z + 1) * width)
        stage[z, 0:width] = q_ref[at]
        stage[z, width:lanes] = gatt[at]
    for j in range(1, hh):
        to = seq_at(reps * j)
        send(stage.at[to // reps], qgbuf.at[j], qg_s.at[j], qg_r.at[j], to, mh)
    qgbuf[0] = stage[my_z]

    offsets = lax.broadcasted_iota(jnp.int32, (1, rows), 1)
    key_pos = jnp.concatenate(
        [order_ref[seq_at(-k)] * rows + offsets for k in range(n)], axis=1
    )
    row_iota = lax.broadcasted_iota(jnp.int32, (rows, 1), 0)
    low = lax.broadcasted_iota(jnp.int32, (rows, lanes), 1) < width

    for step, (i, d) in enumerate(far):
        if step < len(far) // 2:
            forward(i, d)
    for k in range(1, n):
        at = slice(k * rows, (k + 1) * rows)
        arrived(kvbuf.at[pl.ds(k * rows, rows)], kv_s.at[k], kv_r.at[k])
        kvt[:, at] = jnp.transpose(kvbuf[at, :].astype(F32)).astype(BF16)
    ahead = far[len(far) // 2:]

    for j in range(hh):
        owner = seq_at(-reps * j)
        if j > 0:
            arrived(qgbuf.at[j], qg_s.at[j], qg_r.at[j])
        qg = jnp.transpose(qgbuf[j].astype(F32))
        grad_rows = jnp.where(low, 0.0, qg)
        scores = dot(jnp.where(low, qg, 0.0).astype(BF16), kvt[...]) * inv_root
        allowed = key_pos <= order_ref[owner] * rows + row_iota
        scores = jnp.where(allowed, scores, -jnp.inf)
        e = jnp.exp(scores - jnp.max(scores, axis=1, keepdims=True))
        p = (e * (1.0 / jnp.sum(e, axis=1, keepdims=True))).astype(BF16)
        probs[j * rows:(j + 1) * rows, :] = p
        att = dot(p, kvbuf[...])
        dprob = dot(grad_rows.astype(BF16), kvt[...])
        grad_dot = jnp.sum(grad_rows * att.astype(BF16).astype(F32), axis=1, keepdims=True)
        ds = (p.astype(F32) * (dprob - grad_dot)).astype(BF16)
        dscore[j * rows:(j + 1) * rows, :] = ds
        home_out[j] = jnp.transpose(
            jnp.where(low, dot(ds, kvbuf[...]) * inv_root, att)
        ).astype(BF16)
        if j == 0:
            homebuf[my_z] = home_out[0]
        else:
            send(home_out.at[j], homebuf.at[my_z], home_s.at[j], home_r.at[j], owner, mh)
        for i, d in ahead[j * len(ahead) // hh:(j + 1) * len(ahead) // hh]:
            forward(i, d)

    qgt = jnp.concatenate([qgbuf[j] for j in range(hh)], axis=1)
    grad_k = dot(qgt, dscore[...]) * inv_root
    grad_v = dot(qgt, probs[...])
    upper = lax.broadcasted_iota(jnp.int32, (lanes, rows), 0) < width
    for k in [*range(1, n), 0]:
        at = slice(k * rows, (k + 1) * rows)
        dkv_out[k] = jnp.transpose(jnp.where(upper, grad_k[:, at], grad_v[:, at])).astype(BF16)
        if k == 0:
            dkvbuf[0] = dkv_out[0]
        else:
            send(dkv_out.at[k], dkvbuf.at[k], dkv_s.at[k], dkv_r.at[k], seq_at(-k), mh)

    for j in range(1, hh):
        arrived(homebuf.at[lax.rem(my_z + j, hh)], home_s.at[j], home_r.at[j])
    for z in range(hh):
        at = slice(z * width, (z + 1) * width)
        attbuf[0, at, :] = homebuf[z, width:lanes, :]
    for d in range(nh - 1, 0, -1):
        send(attbuf.at[0], attbuf.at[d], att_s.at[d], att_r.at[d], me, head_at(d))
    for z in range(hh):
        dq_ref[z * width:(z + 1) * width, :] = homebuf[z, 0:width, :]

    total = None
    for d in range(nh):
        if d:
            arrived(attbuf.at[d], att_s.at[d], att_r.at[d])
        if d == 0:
            weight = w_ref[:, pl.ds(pl.multiple_of(mh * cols, cols), cols)]
        else:
            if d == 1:
                arrived(wbuf.at[1], w_s.at[1, 0], w_r.at[1, 0])
            else:
                for i in range(PIECES):
                    for r in range(1, reps):
                        source = lax.rem(my_r + (reps - r), reps)
                        arrived(
                            wbuf.at[d, w_part(source, i)], f_s.at[d, i, r], f_r.at[d, i, r]
                        )
            weight = wbuf[d]
        att_rows = jnp.transpose(attbuf[d].astype(F32)).astype(BF16)
        term = dot(att_rows, weight)
        total = term if total is None else total + term
    mixed_ref[...] = total.astype(BF16)

    for k in range(1, n):
        arrived(dkvbuf.at[k], dkv_s.at[k], dkv_r.at[k])
    for z in range(hh):
        acc = None
        for r in range(reps):
            term = dkvbuf[lax.rem(z * reps + r + n - me, n)].astype(F32)
            acc = term if acc is None else acc + term
        dkv_ref[:, z, :] = acc.astype(BF16)

    for copy in sends:
        copy.wait_send()


def fused_local(n, nh, queries, keys_values, out_weight, out_grad, block_order):
    rows, hh, width = queries.shape
    lanes = 2 * width
    depth = out_grad.shape[1]
    cols = depth // nh
    reps = n // hh
    vmem = pl.BlockSpec(memory_space=pltpu.VMEM)
    hbm = pl.BlockSpec(memory_space=pl.ANY)
    dma = pltpu.SemaphoreType.DMA
    mixed, dq, dkv = pl.pallas_call(
        functools.partial(fused, n, nh, hh, rows, width, 1.0 / math.sqrt(width)),
        out_shape=(
            jax.ShapeDtypeStruct((rows, cols), BF16),
            jax.ShapeDtypeStruct((hh * width, rows), BF16),
            jax.ShapeDtypeStruct((rows, hh, lanes), BF16),
        ),
        in_specs=[hbm, hbm, hbm, hbm, pl.BlockSpec(memory_space=pltpu.SMEM)],
        out_specs=(vmem, vmem, vmem),
        scratch_shapes=[
            pltpu.VMEM((hh * width, rows), BF16),
            pltpu.VMEM((rows, hh, lanes), BF16),
            pltpu.VMEM((hh * width, depth), BF16),
            pltpu.VMEM((rows, depth), BF16),
            pltpu.VMEM((hh, rows, lanes), BF16),
            pltpu.VMEM((n * rows, lanes), BF16),
            pltpu.VMEM((lanes, n * rows), BF16),
            pltpu.VMEM((hh, lanes, rows), BF16),
            pltpu.VMEM((hh, lanes, rows), BF16),
            pltpu.VMEM((nh, hh * width, cols), BF16),
            pltpu.VMEM((hh * rows, n * rows), BF16),
            pltpu.VMEM((hh * rows, n * rows), BF16),
            pltpu.VMEM((nh, hh * width, rows), BF16),
            pltpu.VMEM((hh, lanes, rows), BF16),
            pltpu.VMEM((hh, lanes, rows), BF16),
            pltpu.VMEM((n, rows, lanes), BF16),
            pltpu.VMEM((n, rows, lanes), BF16),
            dma((4,)),
            dma((n,)), dma((n,)),
            dma((nh, PIECES)), dma((nh, PIECES)),
            dma((nh, PIECES, reps)), dma((nh, PIECES, reps)),
            dma((hh,)), dma((hh,)),
            dma((nh,)), dma((nh,)),
            dma((hh,)), dma((hh,)),
            dma((n,)), dma((n,)),
        ],
        compiler_params=pltpu.CompilerParams(
            collective_id=0, has_side_effects=True, vmem_limit_bytes=VLIM * 2**16
        ),
    )(
        jnp.transpose(queries, (1, 2, 0)).reshape(hh * width, rows),
        keys_values,
        out_weight.reshape(hh * width, depth),
        out_grad,
        block_order,
    )
    dq = jnp.transpose(dq.reshape(hh, width, rows), (2, 0, 1))
    return mixed, dq, dkv


def log_normalizer(scores, allowed):
    masked = jnp.where(allowed, scores, -jnp.inf)
    row_max = jnp.max(masked, axis=-1, keepdims=True)
    row_total = jnp.sum(jnp.exp(masked - row_max), axis=-1, keepdims=True)
    return (row_max + jnp.log(row_total))[..., 0]


def local(queries, keys_values, out_weight, out_grad, block_order):
    tok_rows = queries.shape[0]
    head_width = queries.shape[2]
    inv_root = 1.0 / math.sqrt(head_width)
    my_block = block_order[lax.axis_index("seq")]
    offsets = jnp.arange(tok_rows, dtype=jnp.int32)
    my_position = my_block * tok_rows + offsets
    all_position = (block_order[:, None] * tok_rows + offsets[None, :]).reshape(-1)
    gathered = lax.all_gather(keys_values, "seq", axis=0, tiled=True)
    all_keys = gathered[:, :, :head_width]
    all_values = gathered[:, :, head_width:]
    allowed = (all_position[None, :] <= my_position[:, None])[None]
    scores = (
        jnp.einsum("qhd,khd->hqk", queries, all_keys, preferred_element_type=jnp.float32) * inv_root
    )
    log_total = log_normalizer(scores, allowed)
    probs_low = jnp.where(allowed, jnp.exp(scores - log_total[:, :, None]), 0.0).astype(
        jnp.bfloat16
    )
    attended = jnp.einsum(
        "hqk,khd->qhd", probs_low, all_values, preferred_element_type=jnp.float32
    ).astype(jnp.bfloat16)
    partial_value = jnp.einsum(
        "qhd,hde->qe", attended, out_weight, preferred_element_type=jnp.float32
    )
    mixed_out = lax.psum_scatter(partial_value, "head", scatter_dimension=1, tiled=True).astype(
        jnp.bfloat16
    )
    grad_att = jnp.einsum(
        "qe,hde->qhd", out_grad, out_weight, preferred_element_type=jnp.float32
    ).astype(jnp.bfloat16)
    grad_dot = jnp.sum(grad_att.astype(jnp.float32) * attended.astype(jnp.float32), axis=2)
    dprob = jnp.einsum("qhd,khd->hqk", grad_att, all_values, preferred_element_type=jnp.float32)
    dscore = (probs_low.astype(jnp.float32) * (dprob - grad_dot.T[:, :, None])).astype(jnp.bfloat16)
    grad_queries = (
        jnp.einsum("hqk,khd->qhd", dscore, all_keys, preferred_element_type=jnp.float32) * inv_root
    ).astype(jnp.bfloat16)
    grad_keys = (
        jnp.einsum("hqk,qhd->khd", dscore, queries, preferred_element_type=jnp.float32) * inv_root
    )
    grad_values = jnp.einsum(
        "hqk,qhd->khd", probs_low, grad_att, preferred_element_type=jnp.float32
    )
    terms = jnp.concatenate([grad_keys, grad_values], axis=2)
    summed = lax.psum_scatter(terms, "seq", scatter_dimension=0, tiled=True)
    grad_keys_values = summed.astype(jnp.bfloat16)
    return (mixed_out, grad_queries, grad_keys_values)


def solution(mesh):
    n, nh = mesh.shape["seq"], mesh.shape["head"]

    def step(queries, keys_values, out_weight, out_grad, block_order):
        rows, hh, width = queries.shape
        fits = nh % 2 == 0 and n % hh == 0 and width == 64 and rows % 128 == 0
        if fits and 8 * n * rows * hh * rows < 2**23:
            return fused_local(n, nh, queries, keys_values, out_weight, out_grad, block_order)
        return local(queries, keys_values, out_weight, out_grad, block_order)

    return jax.shard_map(
        step,
        mesh=mesh,
        in_specs=(
            P("seq", "head", None),
            P("seq", "head", None),
            P("head", None, None),
            P("seq", None),
            P(),
        ),
        out_specs=(P("seq", "head"), P("seq", "head", None), P("seq", "head", None)),
        check_vma=False,
    )
```
